512 devices in a mesh: pipe: 4 (over x), tensor: 32 (over z, y_lo), dp: 4 (over y_hi, core).
Axes of the slice: x: 4, y: 8 (y_hi: 2, y_lo: 4; y = y_hi * 4 + y_lo), z: 8, core: 2. Of those that a mesh axis runs over, the one named last changes fastest.
Arguments:
- stash: bfloat16 [4096, 29568], P(('pipe', 'dp'), 'tensor'), may hold values from -6 to 6
- out_grads: bfloat16 [4096, 8192], P(('pipe', 'dp'), 'tensor'), may hold values from -0.09375 to 0.09375
- block_counts: int32 [16], replicated, may hold values from 1 to 2
Outputs:
- weight_grad: bfloat16 [29568, 8192], P('tensor', ('pipe', 'dp'))
The draws below stay inside these ranges and needn't reach their ends.
Inputs may be any that keep to these rules, and one draw needn't show every extreme that they name: `block_counts`: each micro-batch has at least one live block; some micro-batch has all 2.
All inputs are finite; a program needn't handle non-finite values.
Results may differ from the reference program's by a relative error of at most 0.001.
Values may be sent and summed in bfloat16 or wider, within the bound.
No kernel may reach another device: no remote copies, remote signals or barrier semaphores. Data moves between devices by JAX's collectives and lax.ppermute only.
A program may use at most 64 MiB of HBM per device.

```python
import jax
import jax.numpy as jnp

D = 8192
FF = 29568
ROWBLK = 128
BLK = 2
MROWS = 256
MICRO = 16
ROWS = 4096


def set_ends(array, rng, least, top_value):
    index_at = [jax.random.randint(jax.random.fold_in(rng, axis), (), 0, length) for axis, length in enumerate(array.shape)]
    main_axis = array.shape.index(max(array.shape))
    beside = index_at[:main_axis] + [(index_at[main_axis] + 1) % array.shape[main_axis]] + index_at[main_axis + 1:]
    return array.at[tuple(index_at)].set(least).at[tuple(beside)].set(top_value)


def block_scale(own_key, extent, shards, smallest, top_value):
    factor_of, own = 1.0, jax.random.fold_in(own_key, 6)
    for position, blocks in shards:
        steps = jnp.exp(jax.random.uniform(jax.random.fold_in(own, position), (blocks,), jnp.float32, smallest / len(shards), top_value / len(shards)))
        factor_of = factor_of * jnp.repeat(steps, extent[position] // blocks).reshape([-1 if axis == position else 1 for axis in range(len(extent))])
    return factor_of


def scatter_about(stream_key, extent, scale, reach, cuts=(), kind=jnp.bfloat16):
    drawn = scale * jax.random.normal(stream_key, extent, jnp.float32)
    if cuts:
        drawn = drawn * block_scale(stream_key, extent, cuts, -0.22, 0.18)
    return jnp.clip(drawn, -reach, reach).astype(kind)


def setup_inputs(seed: int = 0) -> dict:
    key_list = jax.random.split(jax.random.key(seed), 4)
    stash = scatter_about(key_list[0], (ROWS, FF), 1.0, 6.0, ((0, 16), (1, 32)))
    out_grads = scatter_about(key_list[1], (ROWS, D), ROWS ** -0.5, 0.09375, ((0, 16), (1, 32)))
    block_counts = set_ends(jax.random.randint(key_list[2], (MICRO,), 1, BLK + 1), jax.random.fold_in(key_list[2], 1), 1, BLK).astype(jnp.int32)
    return dict(stash=stash, out_grads=out_grads, block_counts=block_counts)


def reference(stash, out_grads, block_counts):
    shaped = out_grads.reshape(MICRO, MROWS, D)
    slots = jnp.arange(MROWS, dtype=jnp.int32)
    alive = slots[None, :] < ROWBLK * block_counts[:, None]
    live_grads = jnp.where(alive[:, :, None], shaped, jnp.zeros_like(shaped)).reshape(ROWS, D)
    total = jnp.dot(stash.T, live_grads, preferred_element_type=jnp.float32)
    return total.astype(jnp.bfloat16)
```

```python
import itertools

import jax
import jax.numpy as jnp
from jax import lax
from jax.experimental import pallas as pl
from jax.experimental.pallas import tpu as pltpu
from jax.sharding import Mesh, PartitionSpec as P

ROWBLK = 128
MROWS = 256
NX, NZ, NYL, NYH, NC = 4, 8, 4, 2, 2
ALL = ("x", "z", "yl", "yh", "c")
PLACES = list(itertools.product(range(NX), range(NZ), range(NYL), range(NYH), range(NC)))


def linear(x, z, yl, yh, c):
    return (((x * NZ + z) * NYL + yl) * NYH + yh) * NC + c


def permute(value, target):
    return lax.ppermute(value, ALL, [(linear(*p), linear(*target(*p))) for p in PLACES])


def to_owner_plane(x, z, yl, yh, c):
    return z // 2, z ^ (2 * x + yh), 2 * c + yl % 2, z % 2, yl // 2


def product(zi, own, yh, s_own, s_par, pieces):
    width, rows = s_own.shape[0], 2 * MROWS
    cols = 2 * pieces[0].shape[-1]
    n = len(pieces)

    def kernel(where, s_own_ref, s_par_ref, *refs):
        g_refs, out_ref, s_vm, g_vm, acc, s_sem, g_sem = refs[:n], *refs[n:]
        z0, own0, yh0 = where[0], where[1], where[2]
        copies = []
        for x in range(NX):
            for ref, half in ((s_own_ref, yh0), (s_par_ref, 1 - yh0)):
                q = 2 * x + half
                copy = pltpu.make_async_copy(ref.at[:, pl.ds(x * rows, rows)], s_vm.at[q], s_sem)
                copy.start()
                copies.append(copy)
        for k, ref in enumerate(g_refs):
            for b in range(NYL):
                copy = pltpu.make_async_copy(
                    ref.at[b],
                    g_vm.at[k, pl.ds((b // 2) * MROWS, MROWS), pl.ds((b % 2) * MROWS, MROWS)],
                    g_sem,
                )
                copy.start()
                copies.append(copy)
        for copy in copies:
            copy.wait()
        for k in range(n):
            q = lax.rem(z0 + k, NZ) ^ own0
            part = jnp.dot(s_vm[q], g_vm[k], preferred_element_type=jnp.float32)
            if k == 0:
                acc[...] = part
            elif k < n - 1:
                acc[...] += part
            else:
                out_ref[...] = (acc[...] + part).astype(out_ref.dtype)

    return pl.pallas_call(
        kernel,
        out_shape=jax.ShapeDtypeStruct((width, cols), jnp.bfloat16),
        in_specs=[pl.BlockSpec(memory_space=pltpu.SMEM)] + [pl.BlockSpec(memory_space=pl.ANY)] * (2 + n),
        out_specs=pl.BlockSpec(memory_space=pltpu.VMEM),
        scratch_shapes=[
            pltpu.VMEM((NZ, width, rows), jnp.bfloat16),
            pltpu.VMEM((NZ, rows, cols), jnp.bfloat16),
            pltpu.VMEM((width, cols), jnp.float32),
            pltpu.SemaphoreType.DMA,
            pltpu.SemaphoreType.DMA,
        ],
        compiler_params=pltpu.CompilerParams(vmem_limit_bytes=48 << 20),
        cost_estimate=pl.CostEstimate(flops=2 * width * NZ * rows * cols, bytes_accessed=12 << 20, transcendentals=0),
    )(jnp.stack([zi, own, yh]).astype(jnp.int32), s_own, s_par, *pieces)


def shards(stash, out_grads, block_counts):
    xi, zi, yh, c = (lax.axis_index(a) for a in ("x", "z", "yh", "c"))
    micro = (xi * NYH + yh) * NC + c

    slots = jnp.arange(MROWS, dtype=jnp.int32)
    alive = slots < ROWBLK * block_counts[micro]
    grads = jnp.where(alive[:, None], out_grads, jnp.zeros_like(out_grads))

    near = permute(grads, to_owner_plane)
    partner = lax.ppermute(stash, "yh", [(0, 1), (1, 0)])
    s_own = lax.all_gather(stash, ("x", "c"), axis=0, tiled=True)
    s_par = lax.all_gather(partner, ("x", "c"), axis=0, tiled=True)

    piece = lax.all_gather(near, "yl", axis=0, tiled=False)
    up = [(i, (i + 1) % NZ) for i in range(NZ)]
    down = [(i, (i - 1) % NZ) for i in range(NZ)]
    below, above = [piece], [piece]
    for _ in range(3):
        below.append(lax.ppermute(below[-1], "z", up))
        above.append(lax.ppermute(above[-1], "z", down))
    last = jnp.where(c == 0, below[3], above[3])
    far = permute(last, lambda x, z, yl, yh, c: (x, (z + 1 - 2 * c) % NZ, yl, yh, c))
    pieces = [piece, above[1], above[2], above[3], far, below[3], below[2], below[1]]
    return product(zi, 2 * xi + yh, yh, s_own.T, s_par.T, pieces)


def solution(mesh):
    fine = Mesh(mesh.devices.reshape(NX, NZ, NYL, NYH, NC), ALL)
    rows, features = ("x", "yh", "c"), ("z", "yl")
    placed = (P(rows, features), P(rows, features), P())
    return jax.shard_map(shards, mesh=fine, in_specs=placed, out_specs=P(features, rows), check_vma=False)
```

```python
import itertools

import jax
import jax.numpy as jnp
from jax import lax
from jax.experimental import pallas as pl
from jax.experimental.pallas import tpu as pltpu
from jax.sharding import Mesh, PartitionSpec as P

ROWBLK = 128
MROWS = 256
VMEM = 56 << 20
NX, NZ, NYL, NYH, NC = 4, 8, 4, 2, 2
ALL = ("x", "z", "yl", "yh", "c")
PLACES = list(itertools.product(range(NX), range(NZ), range(NYL), range(NYH), range(NC)))


def linear(x, z, yl, yh, c):
    return (((x * NZ + z) * NYL + yl) * NYH + yh) * NC + c


def permute(value, target):
    return lax.ppermute(value, ALL, [(linear(*p), linear(*target(*p))) for p in PLACES])


def to_owner_plane(x, z, yl, yh, c):
    return z // 2, z ^ (2 * x + yh), 2 * c + yl % 2, z % 2, yl // 2


def other_half(x, z, yl, yh, c):
    return x, z, yl, 1 - yh, c


def other_core(x, z, yl, yh, c):
    return x, z, yl, yh, 1 - c


def product(place, counts, stashes, grads, width):
    rows, cols, pad = 2 * MROWS, 2 * MROWS, stashes[0].shape[1]

    def kernel(place_ref, counts_ref, *refs):
        s_refs, (g_ref, out_ref, s_vm, g_vm, total, s_sem, g_sem) = refs[:4], refs[4:]
        x0, yh0, c0 = (place_ref[i] for i in range(3))
        own = 2 * x0 + yh0

        def stash_copies(x, h):
            q = 2 * x + (yh0 if h == 0 else 1 - yh0)
            return [
                pltpu.make_async_copy(
                    s_refs[2 * h + i].at[x],
                    s_vm.at[q, :, pl.ds(pl.multiple_of((c0 if i == 0 else 1 - c0) * MROWS, MROWS), MROWS)],
                    s_sem.at[q],
                )
                for i in range(NC)
            ]

        def grad_copies(q):
            return [
                pltpu.make_async_copy(
                    g_ref.at[q ^ own, b],
                    g_vm.at[q, pl.ds((b // 2) * MROWS, MROWS), pl.ds((b % 2) * MROWS, MROWS)],
                    g_sem.at[q],
                )
                for b in range(NYL)
            ]

        for q in range(NZ):
            for copy in grad_copies(q):
                copy.start()
            for copy in stash_copies(q // 2, q % 2):
                copy.start()
        for x in range(NX):
            for h in range(NYH):
                for copy in stash_copies(x, h):
                    copy.wait()
        for q in range(NZ):
            for copy in grad_copies(q):
                copy.wait()
            for c in range(NC):
                @pl.when(counts_ref[2 * q + c] < 2)
                def _():
                    g_vm[q, pl.ds(c * MROWS + ROWBLK, ROWBLK), :] = jnp.zeros((ROWBLK, cols), jnp.bfloat16)
            part = jnp.dot(s_vm[q], g_vm[q], preferred_element_type=jnp.float32)
            if q == 0:
                total[...] = part
            elif q < NZ - 1:
                total[...] += part
            else:
                out_ref[...] = (total[...] + part)[:width].astype(jnp.bfloat16)

    return pl.pallas_call(
        kernel,
        out_shape=jax.ShapeDtypeStruct((width, cols), jnp.bfloat16),
        in_specs=[pl.BlockSpec(memory_space=pltpu.SMEM)] * 2 + [pl.BlockSpec(memory_space=pl.ANY)] * 5,
        out_specs=pl.BlockSpec(memory_space=pltpu.VMEM),
        scratch_shapes=[
            pltpu.VMEM((NZ, pad, rows), jnp.bfloat16),
            pltpu.VMEM((NZ, rows, cols), jnp.bfloat16),
            pltpu.VMEM((pad, cols), jnp.float32),
            pltpu.SemaphoreType.DMA((NZ,)),
            pltpu.SemaphoreType.DMA((NZ,)),
        ],
        compiler_params=pltpu.CompilerParams(vmem_limit_bytes=VMEM),
        cost_estimate=pl.CostEstimate(flops=16 * pad * rows * cols, bytes_accessed=13 << 20, transcendentals=0),
    )(place, counts, *stashes, grads)


def together(*values):
    return lax.optimization_barrier(values)


def spread(block, axis, size):
    return lax.all_to_all(jnp.broadcast_to(block, (size, *block.shape)), axis, 0, 0)


def shards(stash, out_grads, block_counts):
    place = jnp.stack([lax.axis_index(a) for a in ("x", "yh", "c")]).astype(jnp.int32)
    width = stash.shape[1]
    own = jnp.pad(stash.T, ((0, -width % 32), (0, 0)))

    near = permute(out_grads, to_owner_plane)
    piece = lax.all_gather(near, "yl", axis=0, tiled=True)
    grads = lax.all_gather(piece, "z", axis=0, tiled=True)

    piece, own = together(piece, own)
    partner = permute(own, other_half)
    own4 = spread(own, "x", NX)
    partner4 = spread(partner, "x", NX)
    stashes = [own4, permute(own4, other_core), partner4, permute(partner4, other_core)]
    return product(place, block_counts, stashes, grads.reshape(NZ, NYL, MROWS, MROWS), width)


def solution(mesh):
    fine = Mesh(mesh.devices.reshape(NX, NZ, NYL, NYH, NC), ALL)
    rows, features = ("x", "yh", "c"), ("z", "yl")
    placed = (P(rows, features), P(rows, features), P())
    return jax.shard_map(shards, mesh=fine, in_specs=placed, out_specs=P(features, rows), check_vma=False)
```

```python
import itertools

import jax
import jax.numpy as jnp
from jax import lax
from jax.experimental import pallas as pl
from jax.experimental.pallas import tpu as pltpu
from jax.sharding import Mesh, PartitionSpec as P

ROWBLK = 128
MROWS = 256
VMEM = 60 << 20
NX, NZ, NYL, NYH, NC = 4, 8, 4, 2, 2
ALL = ("x", "z", "yl", "yh", "c")
PLACES = list(itertools.product(range(NX), range(NZ), range(NYL), range(NYH), range(NC)))


def linear(x, z, yl, yh, c):
    return (((x * NZ + z) * NYL + yl) * NYH + yh) * NC + c


def permute(value, target):
    return lax.ppermute(value, ALL, [(linear(*p), linear(*target(*p))) for p in PLACES])


def to_owner_plane(x, z, yl, yh, c):
    return z // 2, z ^ (2 * x + yh), 2 * c + yl % 2, z % 2, yl // 2


def other_half(x, z, yl, yh, c):
    return x, z, yl, 1 - yh, c


def other_core(x, z, yl, yh, c):
    return x, z, yl, yh, 1 - c


def along_x(steps):
    return lambda x, z, yl, yh, c: ((x + steps) % NX, z, yl, yh, c)


def product(place, counts, stashes, grads, width):
    rows, cols = 2 * MROWS, 2 * MROWS
    arrays = []
    for _, *sides in stashes:
        for _, array in sides:
            if not any(array is a for a in arrays):
                arrays.append(array)
    where_is = [[(i, [array is a for a in arrays].index(True)) for i, array in sides] for _, *sides in stashes]
    keys = [key for key, *_ in stashes]
    pad, ns, ng = arrays[0].shape[-2], len(arrays), len(grads)

    def kernel(place_ref, counts_ref, *refs):
        s_refs, g_refs, (out_ref, s_vm, g_vm, total, s_sem, g_sem) = refs[:ns], refs[ns : ns + ng], refs[ns + ng :]
        x0, z0, yh0, c0 = (place_ref[i] for i in range(4))
        own = 2 * x0 + yh0

        def q_of(j):
            h, back = keys[j]
            return 2 * lax.rem(x0 - back + NX, NX) + (yh0 if h == 0 else 1 - yh0)

        def grad_copies(j, ref):
            return [
                pltpu.make_async_copy(
                    ref.at[b],
                    g_vm.at[j, pl.ds((b // 2) * MROWS, MROWS), pl.ds((b % 2) * MROWS, MROWS)],
                    g_sem.at[j],
                )
                for b in range(NYL)
            ]

        for j in range(len(keys)):
            if ng == 1:
                for copy in grad_copies(j, g_refs[0].at[q_of(j) ^ own]):
                    copy.start()
            else:
                for d in range(NZ):
                    @pl.when((q_of(j) ^ own) == lax.rem(z0 - d * (1 - 2 * c0) + NZ, NZ))
                    def _():
                        for copy in grad_copies(j, g_refs[d]):
                            copy.start()
            for side, (i, n) in enumerate(where_is[j]):
                c = c0 if side == 0 else 1 - c0
                at = s_vm.at[j, :, pl.ds(pl.multiple_of(c * MROWS, MROWS), MROWS)]
                pltpu.make_async_copy(s_refs[n] if i is None else s_refs[n].at[i], at, s_sem.at[j]).start()
        for j in range(len(keys)):
            for copy in grad_copies(j, g_refs[0].at[0] if ng == 1 else g_refs[0]):
                copy.wait()
            for c in range(NC):
                @pl.when(counts_ref[2 * q_of(j) + c] < 2)
                def _():
                    g_vm[j, pl.ds(c * MROWS + ROWBLK, ROWBLK), :] = jnp.zeros((ROWBLK, cols), jnp.bfloat16)
            for c in range(NC):
                at = s_vm.at[j, :, pl.ds(c * MROWS, MROWS)]
                pltpu.make_async_copy(at, at, s_sem.at[j]).wait()
            part = jnp.dot(s_vm[j], g_vm[j], preferred_element_type=jnp.float32)
            if j == 0:
                total[...] = part
            elif j < NZ - 1:
                total[...] += part
            else:
                out_ref[...] = (total[...] + part)[:width].astype(jnp.bfloat16)

    return pl.pallas_call(
        kernel,
        out_shape=jax.ShapeDtypeStruct((width, cols), jnp.bfloat16),
        in_specs=[pl.BlockSpec(memory_space=pltpu.SMEM)] * 2 + [pl.BlockSpec(memory_space=pl.ANY)] * (ns + ng),
        out_specs=pl.BlockSpec(memory_space=pltpu.VMEM),
        scratch_shapes=[
            pltpu.VMEM((NZ, pad, rows), jnp.bfloat16),
            pltpu.VMEM((NZ, rows, cols), jnp.bfloat16),
            pltpu.VMEM((pad, cols), jnp.float32),
            pltpu.SemaphoreType.DMA((NZ,)),
            pltpu.SemaphoreType.DMA((NZ,)),
        ],
        compiler_params=pltpu.CompilerParams(vmem_limit_bytes=VMEM),
        cost_estimate=pl.CostEstimate(flops=16 * pad * rows * cols, bytes_accessed=13 << 20, transcendentals=0),
    )(place, counts, *arrays, *grads)


def together(*values):
    return lax.optimization_barrier(values)


def shards(stash, out_grads, block_counts):
    place = jnp.stack([lax.axis_index(a) for a in ("x", "z", "yh", "c")]).astype(jnp.int32)
    width = stash.shape[1]
    own = jnp.pad(stash.T, ((0, -width % 32), (0, 0)))

    near = permute(out_grads, to_owner_plane)
    near, own = together(near, own)
    piece = lax.all_gather(near, "yl", axis=0, tiled=True)
    grads = [lax.all_gather(piece, "z", axis=0, tiled=True).reshape(NZ, NYL, MROWS, MROWS)]

    piece, own = together(piece, own)
    partner = permute(own, other_half)
    sides = []
    for h, block in enumerate((own, partner)):
        moved = [permute(block, along_x(back)) for back in (1, 3, 2)]
        backs = (0, 1, 3, 2)
        if h == 0:
            mine = jnp.stack([block, *moved])
            theirs = permute(mine, other_core)
            sides += [((h, back), (i, mine), (i, theirs)) for i, back in enumerate(backs)]
        else:
            mine = jnp.stack(moved)
            theirs = permute(mine, other_core)
            sides.append(((h, 0), (None, block), (None, permute(block, other_core))))
            sides += [((h, back), (i, mine), (i, theirs)) for i, back in enumerate(backs[1:])]
    return product(place, block_counts, sides, grads, width)


def solution(mesh):
    fine = Mesh(mesh.devices.reshape(NX, NZ, NYL, NYH, NC), ALL)
    rows, features = ("x", "yh", "c"), ("z", "yl")
    placed = (P(rows, features), P(rows, features), P())
    return jax.shard_map(shards, mesh=fine, in_specs=placed, out_specs=P(features, rows), check_vma=False)
```

```python
import itertools

import jax
import jax.numpy as jnp
from jax import lax
from jax.experimental import pallas as pl
from jax.experimental.pallas import tpu as pltpu
from jax.sharding import Mesh, PartitionSpec as P

ROWBLK = 128
MROWS = 256
VMEM = 60 << 20
AHEAD = 3
NX, NZ, NYL, NYH, NC = 4, 8, 4, 2, 2
ALL = ("x", "z", "yl", "yh", "c")
PLACES = list(itertools.product(range(NX), range(NZ), range(NYL), range(NYH), range(NC)))


def linear(x, z, yl, yh, c):
    return (((x * NZ + z) * NYL + yl) * NYH + yh) * NC + c


def permute(value, target):
    return lax.ppermute(value, ALL, [(linear(*p), linear(*target(*p))) for p in PLACES])


def to_owner_plane(x, z, yl, yh, c):
    return z // 2, z ^ (2 * x + yh), 2 * c + yl % 2, z % 2, yl // 2


def other_half(x, z, yl, yh, c):
    return x, z, yl, 1 - yh, c


def other_core(x, z, yl, yh, c):
    return x, z, yl, yh, 1 - c


def along_x(steps):
    return lambda x, z, yl, yh, c: ((x + steps) % NX, z, yl, yh, c)


def product(place, counts, stashes, grads, width):
    rows, cols = 2 * MROWS, 2 * MROWS
    arrays = []
    for _, *sides in stashes:
        for _, array in sides:
            if not any(array is a for a in arrays):
                arrays.append(array)
    where_is = [[(i, [array is a for a in arrays].index(True)) for i, array in sides] for _, *sides in stashes]
    keys = [key for key, *_ in stashes]
    pad, ns = arrays[0].shape[-2], len(arrays)

    def kernel(place_ref, counts_ref, *refs):
        s_refs, (g_ref, out_ref, s_vm, g_vm, total, s_sem, g_sem) = refs[:ns], refs[ns:]
        x0, yh0, c0 = (place_ref[i] for i in range(3))
        own = 2 * x0 + yh0

        def q_of(j):
            h, back = keys[j]
            return 2 * lax.rem(x0 - back + NX, NX) + (yh0 if h == 0 else 1 - yh0)

        def core_of(side):
            return c0 if side == 0 else 1 - c0

        def grad_copies(j):
            return [
                pltpu.make_async_copy(
                    g_ref.at[q_of(j) ^ own, 2 * core_of(side) + n],
                    g_vm.at[j, pl.ds(side * MROWS, MROWS), pl.ds(n * MROWS, MROWS)],
                    g_sem.at[j],
                )
                for side in range(NC)
                for n in range(2)
            ]

        def fetch(j):
            for copy in grad_copies(j):
                copy.start()
            for side, (i, n) in enumerate(where_is[j]):
                at = s_vm.at[j, :, pl.ds(side * MROWS, MROWS)]
                pltpu.make_async_copy(s_refs[n] if i is None else s_refs[n].at[i], at, s_sem.at[j]).start()

        for j in range(AHEAD):
            fetch(j)
        for j in range(len(keys)):
            if j + AHEAD < len(keys):
                fetch(j + AHEAD)
            for copy in grad_copies(j):
                copy.wait()
            for side in range(NC):
                @pl.when(counts_ref[2 * q_of(j) + core_of(side)] < 2)
                def _():
                    g_vm[j, pl.ds(side * MROWS + ROWBLK, ROWBLK), :] = jnp.zeros((ROWBLK, cols), jnp.bfloat16)
            for c in range(NC):
                at = s_vm.at[j, :, pl.ds(c * MROWS, MROWS)]
                pltpu.make_async_copy(at, at, s_sem.at[j]).wait()
            part = jnp.dot(s_vm[j], g_vm[j], preferred_element_type=jnp.float32)
            if j == 0:
                total[...] = part
            elif j < NZ - 1:
                total[...] += part
            else:
                out_ref[...] = (total[...] + part)[:width].astype(jnp.bfloat16)

    return pl.pallas_call(
        kernel,
        out_shape=jax.ShapeDtypeStruct((width, cols), jnp.bfloat16),
        in_specs=[pl.BlockSpec(memory_space=pltpu.SMEM)] * 2 + [pl.BlockSpec(memory_space=pl.ANY)] * (ns + 1),
        out_specs=pl.BlockSpec(memory_space=pltpu.VMEM),
        scratch_shapes=[
            pltpu.VMEM((NZ, pad, rows), jnp.bfloat16),
            pltpu.VMEM((NZ, rows, cols), jnp.bfloat16),
            pltpu.VMEM((pad, cols), jnp.float32),
            pltpu.SemaphoreType.DMA((NZ,)),
            pltpu.SemaphoreType.DMA((NZ,)),
        ],
        compiler_params=pltpu.CompilerParams(vmem_limit_bytes=VMEM),
        cost_estimate=pl.CostEstimate(flops=16 * pad * rows * cols, bytes_accessed=13 << 20, transcendentals=0),
    )(place, counts, *arrays, grads)


def together(*values):
    return lax.optimization_barrier(values)


def shards(stash, out_grads, block_counts):
    place = jnp.stack([lax.axis_index(a) for a in ("x", "yh", "c")]).astype(jnp.int32)
    width = stash.shape[1]
    own = jnp.pad(stash.T, ((0, -width % 32), (0, 0)))

    near = permute(out_grads, to_owner_plane)
    near, own = together(near, own)
    piece = lax.all_gather(near, "yl", axis=0, tiled=True)
    grads = lax.all_gather(piece, "z", axis=0, tiled=True).reshape(NZ, NYL, MROWS, MROWS)

    piece, own = together(piece, own)
    partner = permute(own, other_half)
    sides = []
    for h, block in enumerate((own, partner)):
        moved = [permute(block, along_x(back)) for back in (1, 3, 2)]
        backs = (0, 1, 3, 2)
        if h == 0:
            mine = jnp.stack([block, *moved])
            theirs = permute(mine, other_core)
            sides += [((h, back), (i, mine), (i, theirs)) for i, back in enumerate(backs)]
        else:
            mine = jnp.stack(moved)
            theirs = permute(mine, other_core)
            sides.append(((h, 0), (None, block), (None, permute(block, other_core))))
            sides += [((h, back), (i, mine), (i, theirs)) for i, back in enumerate(backs[1:])]
    return product(place, block_counts, sides, grads, width)


def solution(mesh):
    fine = Mesh(mesh.devices.reshape(NX, NZ, NYL, NYH, NC), ALL)
    rows, features = ("x", "yh", "c"), ("z", "yl")
    placed = (P(rows, features), P(rows, features), P())
    return jax.shard_map(shards, mesh=fine, in_specs=placed, out_specs=P(features, rows), check_vma=False)
```

```python
import itertools

import jax
import jax.numpy as jnp
from jax import lax
from jax.experimental import pallas as pl
from jax.experimental.pallas import tpu as pltpu
from jax.sharding import Mesh, PartitionSpec as P

ROWBLK = 128
MROWS = 256
VMEM = 60 << 20
AHEAD = 3
NX, NZ, NYL, NYH, NC = 4, 8, 4, 2, 2
ALL = ("x", "z", "yl", "yh", "c")
PLACES = list(itertools.product(range(NX), range(NZ), range(NYL), range(NYH), range(NC)))


def linear(x, z, yl, yh, c):
    return (((x * NZ + z) * NYL + yl) * NYH + yh) * NC + c


def permute(value, target):
    return lax.ppermute(value, ALL, [(linear(*p), linear(*target(*p))) for p in PLACES])


def to_owner_plane(x, z, yl, yh, c):
    return z // 2, z ^ (2 * x + yh), 2 * c + yl % 2, z % 2, yl // 2


def other_half(x, z, yl, yh, c):
    return x, z, yl, 1 - yh, c


def other_core(x, z, yl, yh, c):
    return x, z, yl, yh, 1 - c


def along_x(steps):
    return lambda x, z, yl, yh, c: ((x + steps) % NX, z, yl, yh, c)


def product(place, counts, stashes, grads, width):
    rows, cols = 2 * MROWS, 2 * MROWS
    arrays = []
    for _, *sides in stashes:
        for _, array in sides:
            if not any(array is a for a in arrays):
                arrays.append(array)
    where_is = [[(i, [array is a for a in arrays].index(True)) for i, array in sides] for _, *sides in stashes]
    keys = [key for key, *_ in stashes]
    pad, ns = arrays[0].shape[-2], len(arrays)

    def kernel(place_ref, counts_ref, *refs):
        s_refs, (g_ref, out_ref, s_vm, g_vm, total, s_sem, g_sem) = refs[:ns], refs[ns:]
        x0, yh0, c0 = (place_ref[i] for i in range(3))
        own = 2 * x0 + yh0

        def q_of(j):
            h, back = keys[j]
            return 2 * lax.rem(x0 - back + NX, NX) + (yh0 if h == 0 else 1 - yh0)

        def core_of(side):
            return c0 if side == 0 else 1 - c0

        def core_of(side):
            return c0 if side == 0 else 1 - c0

        def live(j, side):
            return counts_ref[2 * q_of(j) + core_of(side)] >= 2

        def copies(j, side, size):
            i, n = where_is[j][side]
            found = [
                pltpu.make_async_copy(
                    g_ref.at[q_of(j) ^ own, 2 * core_of(side) + h, pl.ds(0, size), :],
                    g_vm.at[j, pl.ds(side * MROWS, size), pl.ds(h * MROWS, MROWS)],
                    g_sem.at[j],
                )
                for h in range(2)
            ]
            source = s_refs[n] if i is None else s_refs[n].at[i]
            at = s_vm.at[j, :, pl.ds(side * MROWS, size)]
            return [*found, pltpu.make_async_copy(source.at[:, pl.ds(0, size)], at, s_sem.at[j])]

        def each(j, side, act):
            for size, chosen in ((MROWS, live(j, side)), (ROWBLK, jnp.logical_not(live(j, side)))):
                @pl.when(chosen)
                def _():
                    for copy in copies(j, side, size):
                        act(copy)

        def fetch(j):
            for side in range(NC):
                each(j, side, lambda copy: copy.start())

                @pl.when(jnp.logical_not(live(j, side)))
                def _():
                    dead = pl.ds(side * MROWS + ROWBLK, ROWBLK)
                    g_vm[j, dead, :] = jnp.zeros((ROWBLK, cols), jnp.bfloat16)
                    s_vm[j, :, dead] = jnp.zeros((pad, ROWBLK), jnp.bfloat16)

        for j in range(AHEAD):
            fetch(j)
        for j in range(len(keys)):
            if j + AHEAD < len(keys):
                fetch(j + AHEAD)
            for side in range(NC):
                each(j, side, lambda copy: copy.wait())
            part = jnp.dot(s_vm[j], g_vm[j], preferred_element_type=jnp.float32)
            if j == 0:
                total[...] = part
            elif j < NZ - 1:
                total[...] += part
            else:
                out_ref[...] = (total[...] + part)[:width].astype(jnp.bfloat16)

    return pl.pallas_call(
        kernel,
        out_shape=jax.ShapeDtypeStruct((width, cols), jnp.bfloat16),
        in_specs=[pl.BlockSpec(memory_space=pltpu.SMEM)] * 2 + [pl.BlockSpec(memory_space=pl.ANY)] * (ns + 1),
        out_specs=pl.BlockSpec(memory_space=pltpu.VMEM),
        scratch_shapes=[
            pltpu.VMEM((NZ, pad, rows), jnp.bfloat16),
            pltpu.VMEM((NZ, rows, cols), jnp.bfloat16),
            pltpu.VMEM((pad, cols), jnp.float32),
            pltpu.SemaphoreType.DMA((NZ,)),
            pltpu.SemaphoreType.DMA((NZ,)),
        ],
        compiler_params=pltpu.CompilerParams(vmem_limit_bytes=VMEM),
        cost_estimate=pl.CostEstimate(flops=16 * pad * rows * cols, bytes_accessed=13 << 20, transcendentals=0),
    )(place, counts, *arrays, grads)


def together(*values):
    return lax.optimization_barrier(values)


def shards(stash, out_grads, block_counts):
    place = jnp.stack([lax.axis_index(a) for a in ("x", "yh", "c")]).astype(jnp.int32)
    width = stash.shape[1]
    own = jnp.pad(stash.T, ((0, -width % 32), (0, 0)))

    near = permute(out_grads, to_owner_plane)
    near, own = together(near, own)
    piece = lax.all_gather(near, "yl", axis=0, tiled=True)
    grads = lax.all_gather(piece, "z", axis=0, tiled=True).reshape(NZ, NYL, MROWS, MROWS)

    piece, own = together(piece, own)
    partner = permute(own, other_half)
    sides = []
    for h, block in enumerate((own, partner)):
        moved = [permute(block, along_x(back)) for back in (1, 3, 2)]
        backs = (0, 1, 3, 2)
        if h == 0:
            mine = jnp.stack([block, *moved])
            theirs = permute(mine, other_core)
            sides += [((h, back), (i, mine), (i, theirs)) for i, back in enumerate(backs)]
        else:
            mine = jnp.stack(moved)
            theirs = permute(mine, other_core)
            sides.append(((h, 0), (None, block), (None, permute(block, other_core))))
            sides += [((h, back), (i, mine), (i, theirs)) for i, back in enumerate(backs[1:])]
    return product(place, block_counts, sides, grads, width)


def solution(mesh):
    fine = Mesh(mesh.devices.reshape(NX, NZ, NYL, NYH, NC), ALL)
    rows, features = ("x", "yh", "c"), ("z", "yl")
    placed = (P(rows, features), P(rows, features), P())
    return jax.shard_map(shards, mesh=fine, in_specs=placed, out_specs=P(features, rows), check_vma=False)
```

```python
import itertools

import jax
import jax.numpy as jnp
from jax import lax
from jax.experimental import pallas as pl
from jax.experimental.pallas import tpu as pltpu
from jax.sharding import Mesh, PartitionSpec as P

ROWBLK = 128
MROWS = 256
VMEM = 60 << 20
AHEAD = 4
NX, NZ, NYL, NYH, NC = 4, 8, 4, 2, 2
ALL = ("x", "z", "yl", "yh", "c")
PLACES = list(itertools.product(range(NX), range(NZ), range(NYL), range(NYH), range(NC)))


def linear(x, z, yl, yh, c):
    return (((x * NZ + z) * NYL + yl) * NYH + yh) * NC + c


def permute(value, target):
    return lax.ppermute(value, ALL, [(linear(*p), linear(*target(*p))) for p in PLACES])


def to_owner_plane(x, z, yl, yh, c):
    return z // 2, z ^ (2 * x + yh), 2 * c + yl % 2, z % 2, yl // 2


def other_half(x, z, yl, yh, c):
    return x, z, yl, 1 - yh, c


def other_core(x, z, yl, yh, c):
    return x, z, yl, yh, 1 - c


def along_x(steps):
    return lambda x, z, yl, yh, c: ((x + steps) % NX, z, yl, yh, c)


def product(place, counts, stashes, grads, width):
    rows, cols = 2 * MROWS, 2 * MROWS
    arrays = []
    for _, *sides in stashes:
        for _, array in sides:
            if not any(array is a for a in arrays):
                arrays.append(array)
    where_is = [[(i, [array is a for a in arrays].index(True)) for i, array in sides] for _, *sides in stashes]
    keys = [key for key, *_ in stashes]
    pad, ns = arrays[0].shape[-2], len(arrays)

    def kernel(place_ref, counts_ref, *refs):
        s_refs, (g_ref, out_ref, s_vm, g_vm, total, s_sem, g_sem) = refs[:ns], refs[ns:]
        x0, yh0, c0 = (place_ref[i] for i in range(3))
        own = 2 * x0 + yh0

        def q_of(j):
            h, back = keys[j]
            return 2 * lax.rem(x0 - back + NX, NX) + (yh0 if h == 0 else 1 - yh0)

        def core_of(side):
            return c0 if side == 0 else 1 - c0

        def core_of(side):
            return c0 if side == 0 else 1 - c0

        def live(j, side):
            return counts_ref[2 * q_of(j) + core_of(side)] >= 2

        def copies(j, side, size):
            i, n = where_is[j][side]
            found = [
                pltpu.make_async_copy(
                    g_ref.at[q_of(j) ^ own, 2 * core_of(side) + h, pl.ds(0, size), :],
                    g_vm.at[j, pl.ds(side * MROWS, size), pl.ds(h * MROWS, MROWS)],
                    g_sem.at[j],
                )
                for h in range(2)
            ]
            source = s_refs[n] if i is None else s_refs[n].at[i]
            at = s_vm.at[j, :, pl.ds(side * MROWS, size)]
            return [*found, pltpu.make_async_copy(source.at[:, pl.ds(0, size)], at, s_sem.at[j])]

        def each(j, side, act):
            for size, chosen in ((MROWS, live(j, side)), (ROWBLK, jnp.logical_not(live(j, side)))):
                @pl.when(chosen)
                def _():
                    for copy in copies(j, side, size):
                        act(copy)

        def fetch(j):
            for side in range(NC):
                each(j, side, lambda copy: copy.start())

                @pl.when(jnp.logical_not(live(j, side)))
                def _():
                    dead = pl.ds(side * MROWS + ROWBLK, ROWBLK)
                    g_vm[j, dead, :] = jnp.zeros((ROWBLK, cols), jnp.bfloat16)
                    s_vm[j, :, dead] = jnp.zeros((pad, ROWBLK), jnp.bfloat16)

        for j in range(AHEAD):
            fetch(j)
        for j in range(len(keys)):
            if j + AHEAD < len(keys):
                fetch(j + AHEAD)
            for side in range(NC):
                each(j, side, lambda copy: copy.wait())
            part = jnp.dot(s_vm[j], g_vm[j], preferred_element_type=jnp.float32)
            if j == 0:
                total[...] = part
            elif j < NZ - 1:
                total[...] += part
            else:
                out_ref[...] = (total[...] + part)[:width].astype(jnp.bfloat16)

    return pl.pallas_call(
        kernel,
        out_shape=jax.ShapeDtypeStruct((width, cols), jnp.bfloat16),
        in_specs=[pl.BlockSpec(memory_space=pltpu.SMEM)] * 2 + [pl.BlockSpec(memory_space=pl.ANY)] * (ns + 1),
        out_specs=pl.BlockSpec(memory_space=pltpu.VMEM),
        scratch_shapes=[
            pltpu.VMEM((NZ, pad, rows), jnp.bfloat16),
            pltpu.VMEM((NZ, rows, cols), jnp.bfloat16),
            pltpu.VMEM((pad, cols), jnp.float32),
            pltpu.SemaphoreType.DMA((NZ,)),
            pltpu.SemaphoreType.DMA((NZ,)),
        ],
        compiler_params=pltpu.CompilerParams(vmem_limit_bytes=VMEM),
        cost_estimate=pl.CostEstimate(flops=16 * pad * rows * cols, bytes_accessed=13 << 20, transcendentals=0),
    )(place, counts, *arrays, grads)


def together(*values):
    return lax.optimization_barrier(values)


def shards(stash, out_grads, block_counts):
    place = jnp.stack([lax.axis_index(a) for a in ("x", "yh", "c")]).astype(jnp.int32)
    width = stash.shape[1]
    own = jnp.pad(stash.T, ((0, -width % 32), (0, 0)))

    near = permute(out_grads, to_owner_plane)
    near, own = together(near, own)
    piece = lax.all_gather(near, "yl", axis=0, tiled=True)
    grads = lax.all_gather(piece, "z", axis=0, tiled=True).reshape(NZ, NYL, MROWS, MROWS)

    piece, own = together(piece, own)
    partner = permute(own, other_half)
    sides = []
    for h, block in enumerate((own, partner)):
        moved = [permute(block, along_x(back)) for back in (1, 3, 2)]
        backs = (0, 1, 3, 2)
        if h == 0:
            mine = jnp.stack([block, *moved])
            theirs = permute(mine, other_core)
            sides += [((h, back), (i, mine), (i, theirs)) for i, back in enumerate(backs)]
        else:
            mine = jnp.stack(moved)
            theirs = permute(mine, other_core)
            sides.append(((h, 0), (None, block), (None, permute(block, other_core))))
            sides += [((h, back), (i, mine), (i, theirs)) for i, back in enumerate(backs[1:])]
    return product(place, block_counts, sides, grads, width)


def solution(mesh):
    fine = Mesh(mesh.devices.reshape(NX, NZ, NYL, NYH, NC), ALL)
    rows, features = ("x", "yh", "c"), ("z", "yl")
    placed = (P(rows, features), P(rows, features), P())
    return jax.shard_map(shards, mesh=fine, in_specs=placed, out_specs=P(features, rows), check_vma=False)
```
